32 devices in a mesh: table: 2 (over x), image: 16 (over z, y, core).
Axes of the slice: x: 2, y: 2, z: 4, core: 2. Of those that a mesh axis runs over, the one named last changes fastest.
Arguments:
- traces: bfloat16 [512, 1920], P(('table', 'image')), may hold values from -6 to 6
- aperture: int32 [512, 4], P(('table', 'image')), may hold values from 0 to 15, all different within a row; in each aligned block of 16 rows (0 to 15, 16 to 31, ...) at most 8 rows name the same one
- bucket: int32 [512], P(('table', 'image')), may hold values from 0 to 3
- table_node: int32 [512, 4], P(('table', 'image')), may hold values from 0 to 15
- entry_gain: bfloat16 [512, 4], P(('table', 'image')), may hold values from 0.5 to 2
- travel: float32 [16, 16, 1024], P('image', None, 'table'), may hold values from 1 to 1918
- spread: float32 [16, 16, 1024], P('image', None, 'table'), may hold values from 0.1 to 1
Outputs:
- image: float32 [16, 1024], P('image', 'table')
The draws below stay inside these ranges and needn't reach their ends.
Inputs may be any that keep to these rules, and one draw needn't show every extreme that they name: `aperture`: each trace names 4 different tiles. Among the 16 traces of one device at most 8 name the same tile, and in every draw some tile is named by exactly 8 of them.
All inputs are finite; a program needn't handle non-finite values.
Results may differ from the reference program's by a relative error of at most 0.0024.
Values may be sent and summed in bfloat16 or wider, within the bound.
A program may use at most 128 MiB of HBM per device.

```python
import math
import jax
import jax.numpy as jnp
import numpy as np
from jax import lax

NS = 1920
TR_DEV = 16
APER = 4
FILTERS = 4
NODES = 16
TILES = 16
CAP = 8
TRACES = 512
CELLS_TILE = 1024
PER_TILE = 128


def touch_ends(drawn, key, smallest, top_value):
    place = [jax.random.randint(jax.random.fold_in(key, axis), (), 0, length) for axis, length in enumerate(drawn.shape)]
    main_axis = drawn.shape.index(max(drawn.shape))
    neighbour = place[:main_axis] + [(place[main_axis] + 1) % drawn.shape[main_axis]] + place[main_axis + 1:]
    return drawn.at[tuple(place)].set(smallest).at[tuple(neighbour)].set(top_value)


def block_levels(rng, dims, split, smallest, top_value):
    level = 1.0
    for dim, shards_of in split:
        steps = jax.random.uniform(jax.random.fold_in(jax.random.fold_in(rng, 6), dim), (shards_of,), jnp.float32, smallest / len(split), top_value / len(split))
        level = level * jnp.repeat(jnp.exp(steps), dims[dim] // shards_of).reshape((-1,) + (1,) * (len(dims) - 1 - dim))
    return level


def deal_out(own_key, own, number, rows, amount, top, reach, slope):
    sequence = jax.random.permutation(own_key, amount)
    packed, usual = portions_of(amount, rows * top, reach, slope, True), portions_of(amount, rows * top, reach, slope, False)
    places = jnp.arange(amount)

    def named(sizes, rotation):
        used = int((sizes > 0).sum())
        fixed = max(1, used // 4)
        passed = fixed + (places - fixed + rotation * (used - fixed)) % max(1, amount - fixed)
        return jnp.zeros((amount,), jnp.int32).at[sequence[jnp.where(places < fixed, places, passed)]].set(jnp.asarray(sizes, jnp.int32))

    sizes = jnp.where(number % 4 == 0, named(packed, number // 4), named(usual, number - number // 4 - 1))
    mixed = jax.random.permutation(jax.random.fold_in(own, 3), amount)
    source_of, sink = mixed[0:amount // 2 * 2:2], mixed[1:amount // 2 * 2:2]
    room = jnp.minimum(sizes[source_of] - 1, reach - sizes[sink]) // 2
    room = jnp.where((source_of == sequence[0]) | (sink == sequence[0]) | (sizes[sink] == 0), 0, jnp.maximum(room, 0))
    passed = jax.random.randint(jax.random.fold_in(own, 4), (amount // 2,), 0, 1 << 20) % (room + 1)
    sizes = sizes.at[source_of].add(-passed).at[sink].add(passed)
    items = jnp.searchsorted(jnp.cumsum(sizes), jnp.arange(rows * top), side="right").astype(jnp.int32)
    listing = items.reshape(top, rows).T
    listing = listing[jax.random.permutation(jax.random.fold_in(own, 1), rows)]
    rotation = jax.random.randint(jax.random.fold_in(own, 2), (rows, 1), 0, top)
    return jnp.take_along_axis(listing, (jnp.arange(top)[None, :] + rotation) % top, axis=1)


def portions_of(amount, total, most, lean, full):
    loads = [(1 << 20) // math.isqrt(rank ** lean) + 1 for rank in range(1, amount + 1)]
    largest = most if full else min(most, max(-(-total // amount), total * loads[0] // sum(loads)))
    least = 1 if total - largest >= amount - 1 else 0
    holding, rest = [largest] + [least] * (amount - 1), total - largest - least * (amount - 1)
    while rest > 0:
        candidates = [i for i in range(1, amount) if holding[i] < largest] or [i for i in range(1, amount) if holding[i] < most]
        pool, left = sum([loads[i] for i in candidates]), rest
        for i in candidates:
            extra = min(most - holding[i], max(1, left * loads[i] // pool), rest)
            holding[i] = holding[i] + extra
            rest = rest - extra
    return np.array(holding)


def scatter_about(rng, dims, scale, limit, cuts=(), dtype=jnp.bfloat16):
    array = jax.random.normal(rng, dims, jnp.float32) * scale
    if len(cuts) > 0:
        array = block_levels(rng, dims, cuts, -0.22, 0.18) * array
    return jnp.clip(array, min=-limit, max=limit).astype(dtype)


def setup_inputs(seed: int = 0) -> dict:
    key_of = jax.random.split(jax.random.key(seed), 8)
    traces = scatter_about(key_of[0], (TRACES, NS), 1.0, 6.0, ((0, 32),))
    aperture_keys = jax.random.split(jax.random.fold_in(key_of[1], 1), TRACES // TR_DEV)
    aperture_turns = jax.random.permutation(jax.random.fold_in(key_of[1], 3), TRACES // TR_DEV)
    aperture = jax.vmap(lambda own, number: deal_out(jax.random.fold_in(key_of[1], 2), own, number, TR_DEV, TILES, APER, CAP, 2))(aperture_keys, aperture_turns).reshape((TRACES, APER))
    bucket = touch_ends(jax.random.randint(key_of[2], (TRACES,), 0, FILTERS), jax.random.fold_in(key_of[2], 1), 0, FILTERS - 1).astype(jnp.int32)
    table_node = touch_ends(jax.random.randint(key_of[3], (TRACES, APER), 0, NODES), jax.random.fold_in(key_of[3], 1), 0, NODES - 1).astype(jnp.int32)
    entry_gain = jnp.clip(jnp.exp(math.log(2.0) - 1.3862944 * jax.random.uniform(key_of[4], (TRACES, APER), jnp.float32) ** block_levels(key_of[4], (TRACES, APER), ((0, 32),), -0.2, 0.2)), 0.5, 2.0).astype(jnp.bfloat16)
    travel = jnp.clip(1.0 + 1917.0 * jax.random.uniform(key_of[5], (TILES, NODES, CELLS_TILE), jnp.float32) ** block_levels(key_of[5], (TILES, NODES, CELLS_TILE), ((0, 16), (2, 2)), -0.2, 0.2), 1.0, 1918.0)
    spread = jnp.clip(jnp.exp(math.log(1.0) - 2.3025851 * jax.random.uniform(key_of[6], (TILES, NODES, CELLS_TILE), jnp.float32) ** block_levels(key_of[6], (TILES, NODES, CELLS_TILE), ((0, 16), (2, 2)), -0.2, 0.2)), 0.1, 1.0)
    return {"traces": traces, "aperture": aperture, "bucket": bucket, "table_node": table_node, "entry_gain": entry_gain, "travel": travel, "spread": spread}


max_lag = 7

def antialias(trace_rows, filter_index):
    half_width = (2 + 2 * filter_index).astype(jnp.float32)[..., None]
    length = trace_rows.shape[-1]
    widths = [(0, 0)] * (trace_rows.ndim - 1) + [(max_lag, max_lag)]
    padded = jnp.pad(trace_rows, widths)
    summed = jnp.zeros(trace_rows.shape, jnp.float32)
    for sample_lag in range(-max_lag, max_lag + 1):
        ramp_weight = jnp.maximum(half_width - abs(sample_lag), 0.0) / (half_width * half_width)
        window = lax.slice_in_dim(padded, max_lag + sample_lag, max_lag + sample_lag + length, axis=trace_rows.ndim - 1)
        summed = summed + ramp_weight * window
    return summed

def interpolate(stack_tile, travel_tile, spread_tile):
    floor_value = jnp.floor(travel_tile)
    fraction = travel_tile - floor_value
    lower_index = floor_value.astype(jnp.int32)
    lower_value = jnp.take_along_axis(stack_tile, lower_index, axis=1)
    upper_value = jnp.take_along_axis(stack_tile, lower_index + 1, axis=1)
    return lax.optimization_barrier(jnp.sum(spread_tile * ((1.0 - fraction) * lower_value + fraction * upper_value), axis=0))

def reference(traces, aperture, bucket, table_node, entry_gain, travel, spread):
    blocks = traces.shape[0] // TR_DEV
    block_traces = traces.reshape(blocks, TR_DEV, NS)
    block_tiles = aperture.reshape(blocks, TR_DEV * APER)
    block_filters = bucket.reshape(blocks, TR_DEV)
    block_nodes = table_node.reshape(blocks, TR_DEV * APER)
    block_gains = entry_gain.reshape(blocks, TR_DEV, APER)

    def accumulate(stack, block):
        trace_rows, row_tiles, row_filters, row_nodes, row_gains = block
        filtered = antialias(trace_rows.astype(jnp.float32), row_filters)
        contribution = (row_gains.astype(jnp.float32)[:, :, None] * filtered[:, None, :]).astype(jnp.bfloat16)
        flat_values = contribution.reshape(TR_DEV * APER, NS).astype(jnp.float32)
        stack = stack.at[row_tiles, row_nodes].add(flat_values)
        return (stack, None)
    initial = jnp.zeros((TILES, NODES, NS), jnp.float32)
    stack, unused = lax.scan(accumulate, initial, (block_traces, block_tiles, block_filters, block_nodes, block_gains))
    image = jax.vmap(interpolate)(stack, travel, spread)
    return image * (1.0 / math.sqrt(PER_TILE))
```

```python
import functools
import math

import jax
import jax.numpy as jnp
from jax import lax
from jax.experimental import pallas as pl
from jax.experimental.pallas import tpu as pltpu
from jax.sharding import PartitionSpec as P

LANES = 128
FILTERS = 4
MAX_LAG = 7
MESH = pl.DeviceIdType.MESH


def split_axis(count):
    if count == 16:
        return (4, 2, 2)
    root = math.isqrt(count)
    if root * root == count:
        return (root, root, 1)
    return (count, 1, 1)


def both(first, second):
    if first is None:
        return second
    if second is None:
        return first
    return jnp.logical_and(first, second)


def guarded(cond, action):
    if cond is None:
        action()
    else:
        pl.when(cond)(action)


def neighbours(size, at):
    if size == 1:
        return []
    if size == 2:
        return [(1, 1 - at, None)]
    return [(1, at + 1, at < size - 1), (-1, at - 1, at > 0)]


def arrivals(size, at):
    if size == 1:
        return []
    if size == 2:
        return [(1, 1 - at, None, 1, None, None)]
    found = []
    for distance in range(1, size):
        for step in (1, -1):
            source = at - step * distance
            valid = source >= 0 if step > 0 else source < size
            onward = at < size - 1 if step > 0 else at > 0
            found.append((distance, source, valid, step, at + step, onward))
    return found


def eye_column(row, count):
    across = lax.broadcasted_iota(jnp.int32, (count, count), 1)
    down = lax.broadcasted_iota(jnp.int32, (count, count), 0)
    return jnp.sum(jnp.where(across == down, row, 0.0), axis=1, keepdims=True)


def selection(aperture, bucket, node, gain, nodes, half):
    count = aperture.shape[1]
    lane = lax.broadcasted_iota(jnp.int32, (count, 2 * half), 1)
    low = lane < half
    tile = jnp.where(low, lane, lane - half).astype(jnp.float32)
    offset = eye_column(bucket.astype(jnp.float32) * nodes, count)
    total = jnp.zeros((count, 2 * half), jnp.float32)
    for a in range(aperture.shape[0]):
        named = eye_column(aperture[a : a + 1].astype(jnp.float32), count)
        row = eye_column(node[a : a + 1].astype(jnp.float32), count) + offset
        weight = eye_column(gain[a : a + 1].astype(jnp.float32), count)
        total = total + jnp.where(named == tile, jnp.where(low, weight, row), 0.0)
    return total


def triangle(bucket, lag):
    half = 2 + 2 * bucket
    return max(half - lag, 0) / (half * half)


def partial_image(stack, upper, travel, spread):
    floor_value = jnp.floor(travel)
    fraction = travel - floor_value
    lower = floor_value.astype(jnp.int32)
    chunk = lax.shift_right_logical(lower, 7)
    inner = jnp.bitwise_and(lower, LANES - 1)
    pieces = []
    for c in range(travel.shape[1] // LANES):
        cells = slice(c * LANES, (c + 1) * LANES)
        here, within = chunk[:, cells], inner[:, cells]
        low = jnp.zeros(here.shape, jnp.float32)
        high = jnp.zeros(here.shape, jnp.float32)
        for k in range(stack.shape[1] // LANES):
            samples = slice(k * LANES, (k + 1) * LANES)
            mine = here == k
            picked = jnp.take_along_axis(stack[:, samples], within, axis=1, mode="promise_in_bounds")
            above = jnp.take_along_axis(upper[:, samples], within, axis=1, mode="promise_in_bounds")
            low = jnp.where(mine, picked, low)
            high = jnp.where(mine, above, high)
        part = fraction[:, cells]
        value = spread[:, cells] * ((1.0 - part) * low + part * high)
        pieces.append(jnp.sum(value, axis=0, keepdims=True))
    return jnp.concatenate(pieces, axis=1)


def kernel(
    sizes, groups, half, scale,
    aperture_ref, bucket_ref, node_ref, gain_ref, traces_ref, travel_ref, spread_ref,
    out_ref,
    blocks, travels, spreads, parts, outgoing,
    send_sem, recv_sem, table_send, table_recv, part_send, part_recv,
):
    size_z, size_y, size_c = sizes
    me = lax.axis_index("image")
    group = lax.axis_index("table")
    z = me // (size_y * size_c)
    y = lax.rem(me // size_c, size_y)
    core = lax.rem(me, size_c)
    count, samples = traces_ref.shape
    nodes = travel_ref.shape[0]
    cells = travel_ref.shape[1]

    def index(at_z, at_y, at_c):
        return (at_z * size_y + at_y) * size_c + at_c

    links_z, links_y, links_c = neighbours(size_z, z), neighbours(size_y, y), neighbours(size_c, core)
    others = [lax.rem(group + r, groups) for r in range(1, groups)]

    barrier = pltpu.get_barrier_semaphore()
    partners = [(index(to, y, core), cond) for _, to, cond in links_z]
    partners += [(index(z, to, core), cond) for _, to, cond in links_y]
    partners += [(index(z, y, to), cond) for _, to, cond in links_c]
    for to, cond in partners:
        guarded(cond, lambda to=to: pl.semaphore_signal(barrier, inc=1, device_id=(group, to), device_id_type=MESH))
    for other in others:
        pl.semaphore_signal(barrier, inc=1, device_id=(other, me), device_id_type=MESH)

    blocks[me, :, :samples] = traces_ref[...]
    blocks[me, :, samples:] = selection(
        aperture_ref[...], bucket_ref[...], node_ref[...], gain_ref[...], nodes, half
    ).astype(jnp.bfloat16)

    expected = len(others) + sum(1 if cond is None else cond.astype(jnp.int32) for _, cond in partners)
    pl.semaphore_wait(barrier, expected)

    started = []

    def send(slot, direction, to, cond, under=None):
        copy = pltpu.make_async_remote_copy(
            src_ref=blocks.at[slot],
            dst_ref=blocks.at[slot],
            send_sem=send_sem.at[direction, slot],
            recv_sem=recv_sem.at[slot],
            device_id=(group, to),
            device_id_type=MESH,
        )
        guarded(cond, copy.start)
        started.append((slot, direction, under, cond))

    def receive(slot):
        pltpu.make_async_remote_copy(
            src_ref=blocks.at[slot],
            dst_ref=blocks.at[slot],
            send_sem=send_sem.at[0, slot],
            recv_sem=recv_sem.at[slot],
            device_id=(group, me),
            device_id_type=MESH,
        ).wait_recv()

    def number(base, step):
        return base if step > 0 else base + 1

    def send_y(slot, under):
        for step, to, cond in links_y:
            send(slot, number(2, step), index(z, to, core), cond, under)

    def send_c(slot, under):
        for step, to, cond in links_c:
            send(slot, number(4, step), index(z, y, to), cond, under)

    for step, to, cond in links_z:
        send(me, number(0, step), index(to, y, core), cond)
    send_y(me, None)
    send_c(me, None)
    table_copies = []
    for r, other in enumerate(others):
        for which, (source, landing) in enumerate(((travel_ref, travels), (spread_ref, spreads))):
            copy = pltpu.make_async_remote_copy(
                src_ref=source,
                dst_ref=landing.at[group],
                send_sem=table_send.at[which, r],
                recv_sem=table_recv.at[which, group],
                device_id=(other, me),
                device_id_type=MESH,
            )
            copy.start()
            table_copies.append(copy)

    events = []
    along_z = [(0, z, None)]
    for distance, source, valid, step, onward, can in arrivals(size_z, z):
        along_z.append((distance, source, valid))

        def came_z(slot=index(source, y, core), valid=valid, step=step, onward=onward, can=can):
            def run():
                receive(slot)
                send(slot, number(0, step), index(onward, y, core), can, valid)
                send_y(slot, valid)
                send_c(slot, valid)

            guarded(valid, run)

        events.append((distance, 0, came_z))
    for far, source_z, valid_z in along_z:
        for distance, source, valid, step, onward, can in arrivals(size_y, y):

            def came_y(
                slot=index(source_z, source, core),
                valid=both(valid_z, valid), step=step, onward=onward, can=can,
            ):
                def run():
                    receive(slot)
                    if onward is not None:
                        send(slot, number(2, step), index(z, onward, core), can, valid)
                    send_c(slot, valid)

                guarded(valid, run)

            events.append((far + distance, 1, came_y))
    for _, _, run in sorted(events, key=lambda e: e[:2]):
        run()
    for _, source, valid, _, _, _ in arrivals(size_c, core):
        for at_z in range(size_z):
            for at_y in range(size_y):
                receive(index(at_z, at_y, source))

    total = size_z * size_y * size_c * count
    chosen = blocks[:, :, samples:].reshape(total, 2 * half).astype(jnp.float32)
    lane = lax.broadcasted_iota(jnp.int32, (1, 2 * half), 1)
    weight = jnp.sum(jnp.where(lane == me, chosen, 0.0), axis=1, keepdims=True)
    row = jnp.sum(jnp.where(lane == me + half, chosen, 0.0), axis=1, keepdims=True)
    rows = lax.broadcasted_iota(jnp.int32, (1, FILTERS * nodes), 1).astype(jnp.float32)
    member = jnp.where(row == rows, weight, 0.0).astype(jnp.bfloat16)
    stacked = lax.dot_general(
        member,
        blocks[:, :, :samples].reshape(total, samples),
        (((0,), (0,)), ((), ())),
        preferred_element_type=jnp.float32,
    )
    width = samples + LANES
    stacked = jnp.concatenate([stacked, jnp.zeros((FILTERS * nodes, LANES), jnp.float32)], axis=1)
    by_bucket = [stacked[b * nodes : (b + 1) * nodes] for b in range(FILTERS)]
    stack = None
    for lag in range(MAX_LAG + 1):
        mixed = None
        for b in range(FILTERS):
            if (level := triangle(b, lag)) > 0:
                term = by_bucket[b] * level
                mixed = term if mixed is None else mixed + term
        if lag == 0:
            stack = mixed
        else:
            stack = stack + (pltpu.roll(mixed, lag, 1) + pltpu.roll(mixed, width - lag, 1))
    upper = pltpu.roll(stack, width - 1, 1)[:, :samples]
    stack = stack[:, :samples]

    part_copies = []
    for r, other in enumerate(others):
        for which, landing in enumerate((travels, spreads)):
            pltpu.make_async_remote_copy(
                src_ref=landing.at[other],
                dst_ref=landing.at[other],
                send_sem=table_send.at[which, r],
                recv_sem=table_recv.at[which, other],
                device_id=(other, me),
                device_id_type=MESH,
            ).wait_recv()
        outgoing[r] = partial_image(stack, upper, travels[other], spreads[other])
        copy = pltpu.make_async_remote_copy(
            src_ref=outgoing.at[r],
            dst_ref=parts.at[group],
            send_sem=part_send.at[r],
            recv_sem=part_recv.at[group],
            device_id=(other, me),
            device_id_type=MESH,
        )
        copy.start()
        part_copies.append(copy)
    image = partial_image(stack, upper, travel_ref[...], spread_ref[...])
    for slot, direction, under, cond in started:
        copy = pltpu.make_async_remote_copy(
            src_ref=blocks.at[slot],
            dst_ref=blocks.at[slot],
            send_sem=send_sem.at[direction, slot],
            recv_sem=recv_sem.at[slot],
            device_id=(group, me),
            device_id_type=MESH,
        )
        guarded(both(under, cond), copy.wait_send)
    for copy in table_copies:
        copy.wait_send()
    for r, other in enumerate(others):
        pltpu.make_async_remote_copy(
            src_ref=outgoing.at[r],
            dst_ref=parts.at[other],
            send_sem=part_send.at[r],
            recv_sem=part_recv.at[other],
            device_id=(other, me),
            device_id_type=MESH,
        ).wait_recv()
        image = image + parts[other]
    for copy in part_copies:
        copy.wait_send()
    out_ref[...] = image * scale


def per_device(traces, aperture, bucket, table_node, entry_gain, travel, spread):
    tiles = lax.axis_size("image")
    groups = lax.axis_size("table")
    count, samples = traces.shape
    nodes, cells = travel.shape[1], travel.shape[2]
    half = -(-tiles // (LANES // 2)) * (LANES // 2)
    scale = 1.0 / math.sqrt(count * groups * aperture.shape[1])
    vmem = pl.BlockSpec(memory_space=pltpu.VMEM)
    return pl.pallas_call(
        functools.partial(kernel, split_axis(tiles), groups, half, scale),
        out_shape=jax.ShapeDtypeStruct((1, cells), jnp.float32),
        in_specs=[vmem] * 7,
        out_specs=vmem,
        scratch_shapes=[
            pltpu.VMEM((tiles, count, samples + 2 * half), jnp.bfloat16),
            pltpu.VMEM((groups, nodes, cells), jnp.float32),
            pltpu.VMEM((groups, nodes, cells), jnp.float32),
            pltpu.VMEM((groups, 1, cells), jnp.float32),
            pltpu.VMEM((max(groups - 1, 1), 1, cells), jnp.float32),
            pltpu.SemaphoreType.DMA((6, tiles)),
            pltpu.SemaphoreType.DMA((tiles,)),
            pltpu.SemaphoreType.DMA((2, max(groups - 1, 1))),
            pltpu.SemaphoreType.DMA((2, groups)),
            pltpu.SemaphoreType.DMA((max(groups - 1, 1),)),
            pltpu.SemaphoreType.DMA((groups,)),
        ],
        compiler_params=pltpu.CompilerParams(
            collective_id=0, has_side_effects=True, vmem_limit_bytes=48 * 1024 * 1024
        ),
        cost_estimate=pl.CostEstimate(flops=10**8, bytes_accessed=10**6, transcendentals=0),
    )(aperture.T, bucket.reshape(1, count), table_node.T, entry_gain.T, traces, travel[0], spread[0])


def solution(mesh):
    in_specs = (
        P(("table", "image"), None),
        P(("table", "image"), None),
        P(("table", "image")),
        P(("table", "image"), None),
        P(("table", "image"), None),
        P("image", None, "table"),
        P("image", None, "table"),
    )
    out_specs = P("image", "table")
    return jax.shard_map(
        per_device, mesh=mesh, in_specs=in_specs, out_specs=out_specs, check_vma=False
    )
```

```python
import functools
import math

import jax
import jax.numpy as jnp
from jax import lax
from jax.experimental import pallas as pl
from jax.experimental.pallas import tpu as pltpu
from jax.sharding import PartitionSpec as P

LANES = 128
FILTERS = 4
MAX_LAG = 7
MESH = pl.DeviceIdType.MESH


def split_axis(count):
    if count == 16:
        return (4, 2, 2)
    root = math.isqrt(count)
    if root * root == count:
        return (root, root, 1)
    return (count, 1, 1)


def both(first, second):
    if first is None:
        return second
    if second is None:
        return first
    return jnp.logical_and(first, second)


def guarded(cond, action):
    if cond is None:
        action()
    else:
        pl.when(cond)(action)


def neighbours(size, at):
    if size == 1:
        return []
    if size == 2:
        return [(1, 1 - at, None)]
    return [(1, at + 1, at < size - 1), (-1, at - 1, at > 0)]


def arrivals(size, at):
    if size == 1:
        return []
    if size == 2:
        return [(1, 1 - at, None, 1, None, None)]
    found = []
    for distance in range(1, size):
        for step in (1, -1):
            source = at - step * distance
            valid = source >= 0 if step > 0 else source < size
            onward = at < size - 1 if step > 0 else at > 0
            found.append((distance, source, valid, step, at + step, onward))
    return found


def eye_column(row, count):
    across = lax.broadcasted_iota(jnp.int32, (count, count), 1)
    down = lax.broadcasted_iota(jnp.int32, (count, count), 0)
    return jnp.sum(jnp.where(across == down, row, 0.0), axis=1, keepdims=True)


def selection(aperture, bucket, node, gain, nodes, half):
    count = aperture.shape[1]
    lane = lax.broadcasted_iota(jnp.int32, (count, 2 * half), 1)
    low = lane < half
    tile = jnp.where(low, lane, lane - half).astype(jnp.float32)
    offset = eye_column(bucket.astype(jnp.float32) * nodes, count)
    total = jnp.zeros((count, 2 * half), jnp.float32)
    for a in range(aperture.shape[0]):
        named = eye_column(aperture[a : a + 1].astype(jnp.float32), count)
        row = eye_column(node[a : a + 1].astype(jnp.float32), count) + offset
        weight = eye_column(gain[a : a + 1].astype(jnp.float32), count)
        total = total + jnp.where(named == tile, jnp.where(low, weight, row), 0.0)
    return total


def triangle(bucket, lag):
    half = 2 + 2 * bucket
    return max(half - lag, 0) / (half * half)


def partial_image(stack, upper, travel, spread):
    floor_value = jnp.floor(travel)
    fraction = travel - floor_value
    lower = floor_value.astype(jnp.int32)
    chunk = lax.shift_right_logical(lower, 7)
    inner = jnp.bitwise_and(lower, LANES - 1)
    pieces = []
    for c in range(travel.shape[1] // LANES):
        cells = slice(c * LANES, (c + 1) * LANES)
        here, within = chunk[:, cells], inner[:, cells]
        low = jnp.zeros(here.shape, jnp.float32)
        high = jnp.zeros(here.shape, jnp.float32)
        for k in range(stack.shape[1] // LANES):
            samples = slice(k * LANES, (k + 1) * LANES)
            mine = here == k
            picked = jnp.take_along_axis(stack[:, samples], within, axis=1, mode="promise_in_bounds")
            above = jnp.take_along_axis(upper[:, samples], within, axis=1, mode="promise_in_bounds")
            low = jnp.where(mine, picked, low)
            high = jnp.where(mine, above, high)
        part = fraction[:, cells]
        value = spread[:, cells] * ((1.0 - part) * low + part * high)
        pieces.append(jnp.sum(value, axis=0, keepdims=True))
    return jnp.concatenate(pieces, axis=1)


def kernel(
    sizes, groups, half, scale,
    aperture_hbm, bucket_hbm, node_hbm, gain_hbm, traces_ref, travel_ref, spread_ref,
    out_ref,
    aperture_ref, bucket_ref, node_ref, gain_ref,
    blocks, travels, spreads, parts, outgoing, total_ref,
    load_sem, send_sem, recv_sem, table_send, table_recv, part_send, part_recv,
):
    size_z, size_y, size_c = sizes
    me = lax.axis_index("image")
    group = lax.axis_index("table")
    z = me // (size_y * size_c)
    y = lax.rem(me // size_c, size_y)
    core = lax.rem(me, size_c)
    count, samples = traces_ref.shape
    nodes = travel_ref.shape[0]
    cells = travel_ref.shape[1]

    def index(at_z, at_y, at_c):
        return (at_z * size_y + at_y) * size_c + at_c

    loads = [
        pltpu.make_async_copy(source, landing, load_sem.at[k])
        for k, (source, landing) in enumerate((
            (aperture_hbm, aperture_ref), (bucket_hbm, bucket_ref), (node_hbm, node_ref), (gain_hbm, gain_ref),
            (traces_ref, blocks.at[me, :, pl.ds(0, samples)]),
            (travel_ref, travels.at[group]), (spread_ref, spreads.at[group]),
        ))
    ]
    for load in loads:
        load.start()

    links_z, links_y, links_c = neighbours(size_z, z), neighbours(size_y, y), neighbours(size_c, core)
    others = [lax.rem(group + r, groups) for r in range(1, groups)]

    barrier = pltpu.get_barrier_semaphore()
    partners = [(index(to, y, core), cond) for _, to, cond in links_z]
    partners += [(index(z, to, core), cond) for _, to, cond in links_y]
    partners += [(index(z, y, to), cond) for _, to, cond in links_c]
    for to, cond in partners:
        guarded(cond, lambda to=to: pl.semaphore_signal(barrier, inc=1, device_id=(group, to), device_id_type=MESH))
    for other in others:
        pl.semaphore_signal(barrier, inc=1, device_id=(other, me), device_id_type=MESH)

    with jax.named_scope("selection"):
        for load in loads[:4]:
            load.wait()
        blocks[me, :, samples:] = selection(
            aperture_ref[...], bucket_ref[...], node_ref[...], gain_ref[...], nodes, half
        ).astype(jnp.bfloat16)
        loads[4].wait()

    expected = len(others) + sum(1 if cond is None else cond.astype(jnp.int32) for _, cond in partners)
    with jax.named_scope("entry_barrier"):
        pl.semaphore_wait(barrier, expected)

    started = []

    def send(slot, direction, to, cond, under=None):
        copy = pltpu.make_async_remote_copy(
            src_ref=blocks.at[slot],
            dst_ref=blocks.at[slot],
            send_sem=send_sem.at[direction, slot],
            recv_sem=recv_sem.at[slot],
            device_id=(group, to),
            device_id_type=MESH,
        )
        guarded(cond, copy.start)
        started.append((slot, direction, under, cond))

    def receive(slot):
        pltpu.make_async_remote_copy(
            src_ref=blocks.at[slot],
            dst_ref=blocks.at[slot],
            send_sem=send_sem.at[0, slot],
            recv_sem=recv_sem.at[slot],
            device_id=(group, me),
            device_id_type=MESH,
        ).wait_recv()

    def number(base, step):
        return base if step > 0 else base + 1

    def send_y(slot, under):
        for step, to, cond in links_y:
            send(slot, number(2, step), index(z, to, core), cond, under)

    def send_c(slot, under):
        for step, to, cond in links_c:
            send(slot, number(4, step), index(z, y, to), cond, under)

    for step, to, cond in links_z:
        send(me, number(0, step), index(to, y, core), cond)
    send_y(me, None)
    send_c(me, None)
    table_copies = []
    for load in loads[5:]:
        load.wait()
    for r, other in enumerate(others):
        for which, (source, landing) in enumerate(((travel_ref, travels), (spread_ref, spreads))):
            copy = pltpu.make_async_remote_copy(
                src_ref=source,
                dst_ref=landing.at[group],
                send_sem=table_send.at[which, r],
                recv_sem=table_recv.at[which, group],
                device_id=(other, me),
                device_id_type=MESH,
            )
            copy.start()
            table_copies.append(copy)

    plane = size_y * size_c
    total = plane * count

    def add_plane(at_z, first):
        mine = pl.ds(at_z * plane, plane)
        chosen = blocks[mine, :, samples:].reshape(total, 2 * half).astype(jnp.float32)
        lane = lax.broadcasted_iota(jnp.int32, (1, 2 * half), 1)
        weight = jnp.sum(jnp.where(lane == me, chosen, 0.0), axis=1, keepdims=True)
        row = jnp.sum(jnp.where(lane == me + half, chosen, 0.0), axis=1, keepdims=True)
        rows = lax.broadcasted_iota(jnp.int32, (1, FILTERS * nodes), 1).astype(jnp.float32)
        member = jnp.where(row == rows, weight, 0.0).astype(jnp.bfloat16)
        added = lax.dot_general(
            member,
            blocks[mine, :, :samples].reshape(total, samples),
            (((0,), (0,)), ((), ())),
            preferred_element_type=jnp.float32,
        )
        if first:
            total_ref[...] = added
        else:
            total_ref[...] += added

    events = []
    along_z = [(0, z, None)]
    for distance, source, valid, step, onward, can in arrivals(size_z, z):
        along_z.append((distance, source, valid))

        def came_z(slot=index(source, y, core), valid=valid, step=step, onward=onward, can=can):
            def run():
                receive(slot)
                send(slot, number(0, step), index(onward, y, core), can, valid)
                send_y(slot, valid)
                send_c(slot, valid)

            guarded(valid, run)

        events.append((distance, 0, came_z, "from_z_%d" % distance))
    last_y = size_y - 1
    for far, source_z, valid_z in along_z:
        for distance, source, valid, step, onward, can in arrivals(size_y, y):

            def came_y(
                slot=index(source_z, source, core),
                valid=both(valid_z, valid), step=step, onward=onward, can=can,
            ):
                def run():
                    receive(slot)
                    if onward is not None:
                        send(slot, number(2, step), index(z, onward, core), can, valid)
                    send_c(slot, valid)

                guarded(valid, run)

            events.append((far + distance, 1, came_y, "from_y_%d" % far))

        def whole(source_z=source_z, valid_z=valid_z, first=far == 0):
            def run():
                for _, source, _, _, _, _ in arrivals(size_c, core):
                    for at_y in range(size_y):
                        receive(index(source_z, at_y, source))
                add_plane(source_z, first)

            guarded(valid_z, run)

        events.append((far + last_y + 1, 2, whole, "plane_%d" % far))
    for _, _, run, name in sorted(events, key=lambda e: e[:2]):
        with jax.named_scope(name):
            run()
    stacked = total_ref[...]
    with jax.named_scope("triangle_filter"):
        width = samples + LANES
        stacked = jnp.concatenate([stacked, jnp.zeros((FILTERS * nodes, LANES), jnp.float32)], axis=1)
        by_bucket = [stacked[b * nodes : (b + 1) * nodes] for b in range(FILTERS)]
        stack = None
        for lag in range(MAX_LAG + 1):
            mixed = None
            for b in range(FILTERS):
                if (level := triangle(b, lag)) > 0:
                    term = by_bucket[b] * level
                    mixed = term if mixed is None else mixed + term
            if lag == 0:
                stack = mixed
            else:
                stack = stack + (pltpu.roll(mixed, lag, 1) + pltpu.roll(mixed, width - lag, 1))
        upper = pltpu.roll(stack, width - 1, 1)[:, :samples]
        stack = stack[:, :samples]

    with jax.named_scope("other_image"):
        part_copies = []
        for r, other in enumerate(others):
            for which, landing in enumerate((travels, spreads)):
                pltpu.make_async_remote_copy(
                    src_ref=landing.at[other],
                    dst_ref=landing.at[other],
                    send_sem=table_send.at[which, r],
                    recv_sem=table_recv.at[which, other],
                    device_id=(other, me),
                    device_id_type=MESH,
                ).wait_recv()
            outgoing[r] = partial_image(stack, upper, travels[other], spreads[other])
            copy = pltpu.make_async_remote_copy(
                src_ref=outgoing.at[r],
                dst_ref=parts.at[group],
                send_sem=part_send.at[r],
                recv_sem=part_recv.at[group],
                device_id=(other, me),
                device_id_type=MESH,
            )
            copy.start()
            part_copies.append(copy)
    with jax.named_scope("own_image"):
        image = partial_image(stack, upper, travels[group], spreads[group])
    with jax.named_scope("last_waits"):
        for slot, direction, under, cond in started:
            copy = pltpu.make_async_remote_copy(
                src_ref=blocks.at[slot],
                dst_ref=blocks.at[slot],
                send_sem=send_sem.at[direction, slot],
                recv_sem=recv_sem.at[slot],
                device_id=(group, me),
                device_id_type=MESH,
            )
            guarded(both(under, cond), copy.wait_send)
        for copy in table_copies:
            copy.wait_send()
        for r, other in enumerate(others):
            pltpu.make_async_remote_copy(
                src_ref=outgoing.at[r],
                dst_ref=parts.at[other],
                send_sem=part_send.at[r],
                recv_sem=part_recv.at[other],
                device_id=(other, me),
                device_id_type=MESH,
            ).wait_recv()
            image = image + parts[other]
        for copy in part_copies:
            copy.wait_send()
    out_ref[...] = image * scale


def per_device(traces, aperture, bucket, table_node, entry_gain, travel, spread):
    tiles = lax.axis_size("image")
    groups = lax.axis_size("table")
    count, samples = traces.shape
    nodes, cells = travel.shape[1], travel.shape[2]
    half = -(-tiles // (LANES // 2)) * (LANES // 2)
    scale = 1.0 / math.sqrt(count * groups * aperture.shape[1])
    vmem = pl.BlockSpec(memory_space=pltpu.VMEM)
    whole = pl.BlockSpec(memory_space=pl.ANY)
    return pl.pallas_call(
        functools.partial(kernel, split_axis(tiles), groups, half, scale),
        out_shape=jax.ShapeDtypeStruct((1, cells), jnp.float32),
        in_specs=[whole] * 7,
        out_specs=vmem,
        scratch_shapes=[
            pltpu.VMEM(aperture.shape[::-1], jnp.int32),
            pltpu.VMEM((1, count), jnp.int32),
            pltpu.VMEM(table_node.shape[::-1], jnp.int32),
            pltpu.VMEM(entry_gain.shape[::-1], jnp.bfloat16),
            pltpu.VMEM((tiles, count, samples + 2 * half), jnp.bfloat16),
            pltpu.VMEM((groups, nodes, cells), jnp.float32),
            pltpu.VMEM((groups, nodes, cells), jnp.float32),
            pltpu.VMEM((groups, 1, cells), jnp.float32),
            pltpu.VMEM((max(groups - 1, 1), 1, cells), jnp.float32),
            pltpu.VMEM((FILTERS * nodes, samples), jnp.float32),
            pltpu.SemaphoreType.DMA((7,)),
            pltpu.SemaphoreType.DMA((6, tiles)),
            pltpu.SemaphoreType.DMA((tiles,)),
            pltpu.SemaphoreType.DMA((2, max(groups - 1, 1))),
            pltpu.SemaphoreType.DMA((2, groups)),
            pltpu.SemaphoreType.DMA((max(groups - 1, 1),)),
            pltpu.SemaphoreType.DMA((groups,)),
        ],
        compiler_params=pltpu.CompilerParams(
            collective_id=0, has_side_effects=True, vmem_limit_bytes=56 * 1024 * 1024
        ),
        cost_estimate=pl.CostEstimate(flops=10**8, bytes_accessed=10**6, transcendentals=0),
    )(aperture.T, bucket.reshape(1, count), table_node.T, entry_gain.T, traces, travel[0], spread[0])


def solution(mesh):
    in_specs = (
        P(("table", "image"), None),
        P(("table", "image"), None),
        P(("table", "image")),
        P(("table", "image"), None),
        P(("table", "image"), None),
        P("image", None, "table"),
        P("image", None, "table"),
    )
    out_specs = P("image", "table")
    return jax.shard_map(
        per_device, mesh=mesh, in_specs=in_specs, out_specs=out_specs, check_vma=False
    )
```

```python
import functools
import math

import jax
import jax.numpy as jnp
from jax import lax
from jax.experimental import pallas as pl
from jax.experimental.pallas import tpu as pltpu
from jax.sharding import PartitionSpec as P

LANES = 128
FILTERS = 4
MAX_LAG = 7
MESH = pl.DeviceIdType.MESH


def split_axis(count):
    if count == 16:
        return (4, 2, 2)
    root = math.isqrt(count)
    if root * root == count:
        return (root, root, 1)
    return (count, 1, 1)


def peers(size, at):
    found = []
    for step in range(1, size):
        if size & (size - 1):
            found.append(lax.rem(at + step, size))
            continue
        to, bit = at, 1
        while bit <= step:
            if step & bit:
                to = to + bit * (1 - 2 * lax.rem(to // bit, 2))
            bit *= 2
        found.append(to)
    return found


def eye_column(row, count):
    across = lax.broadcasted_iota(jnp.int32, (count, count), 1)
    down = lax.broadcasted_iota(jnp.int32, (count, count), 0)
    return jnp.sum(jnp.where(across == down, row, 0.0), axis=1, keepdims=True)


def selection(aperture, bucket, node, gain, nodes, half):
    count = aperture.shape[1]
    lane = lax.broadcasted_iota(jnp.int32, (count, 2 * half), 1)
    low = lane < half
    tile = jnp.where(low, lane, lane - half).astype(jnp.float32)
    offset = eye_column(bucket.astype(jnp.float32) * nodes, count)
    total = jnp.zeros((count, 2 * half), jnp.float32)
    for a in range(aperture.shape[0]):
        named = eye_column(aperture[a : a + 1].astype(jnp.float32), count)
        row = eye_column(node[a : a + 1].astype(jnp.float32), count) + offset
        weight = eye_column(gain[a : a + 1].astype(jnp.float32), count)
        total = total + jnp.where(named == tile, jnp.where(low, weight, row), 0.0)
    return total


def triangle(bucket, lag):
    half = 2 + 2 * bucket
    return max(half - lag, 0) / (half * half)


def partial_image(stack, upper, travel, spread):
    floor_value = jnp.floor(travel)
    fraction = travel - floor_value
    lower = floor_value.astype(jnp.int32)
    chunk = lax.shift_right_logical(lower, 7)
    inner = jnp.bitwise_and(lower, LANES - 1)
    pieces = []
    for c in range(travel.shape[1] // LANES):
        cells = slice(c * LANES, (c + 1) * LANES)
        here, within = chunk[:, cells], inner[:, cells]
        low = jnp.zeros(here.shape, jnp.float32)
        high = jnp.zeros(here.shape, jnp.float32)
        for k in range(stack.shape[1] // LANES):
            samples = slice(k * LANES, (k + 1) * LANES)
            mine = here == k
            picked = jnp.take_along_axis(stack[:, samples], within, axis=1, mode="promise_in_bounds")
            above = jnp.take_along_axis(upper[:, samples], within, axis=1, mode="promise_in_bounds")
            low = jnp.where(mine, picked, low)
            high = jnp.where(mine, above, high)
        part = fraction[:, cells]
        value = spread[:, cells] * ((1.0 - part) * low + part * high)
        pieces.append(jnp.sum(value, axis=0, keepdims=True))
    return jnp.concatenate(pieces, axis=1)


def kernel(
    sizes, groups, half, scale,
    aperture_hbm, bucket_hbm, node_hbm, gain_hbm, traces_ref, travel_ref, spread_ref,
    out_ref,
    aperture_ref, bucket_ref, node_ref, gain_ref,
    blocks, travels, spreads, parts, outgoing, total_ref,
    load_sem, send_sem, recv_sem, table_send, table_recv, part_send, part_recv,
):
    size_z, size_y, size_c = sizes
    me = lax.axis_index("image")
    group = lax.axis_index("table")
    z = me // (size_y * size_c)
    y = lax.rem(me // size_c, size_y)
    core = lax.rem(me, size_c)
    count, samples = traces_ref.shape
    nodes = travel_ref.shape[0]
    cells = travel_ref.shape[1]

    def index(at_z, at_y, at_c):
        return (at_z * size_y + at_y) * size_c + at_c

    loads = [
        pltpu.make_async_copy(source, landing, load_sem.at[k])
        for k, (source, landing) in enumerate((
            (aperture_hbm, aperture_ref), (bucket_hbm, bucket_ref), (node_hbm, node_ref), (gain_hbm, gain_ref),
            (traces_ref, blocks.at[me, :, pl.ds(0, samples)]),
            (travel_ref, travels.at[group]), (spread_ref, spreads.at[group]),
        ))
    ]
    for load in loads:
        load.start()

    line_z, line_y, line_c = peers(size_z, z), peers(size_y, y), peers(size_c, core)
    others = [lax.rem(group + r, groups) for r in range(1, groups)]

    barrier = pltpu.get_barrier_semaphore()
    partners = [(group, index(to, y, core)) for to in line_z]
    partners += [(group, index(z, to, core)) for to in line_y]
    partners += [(group, index(z, y, to)) for to in line_c]
    partners += [(other, me) for other in others]
    for partner in partners:
        pl.semaphore_signal(barrier, inc=1, device_id=partner, device_id_type=MESH)

    with jax.named_scope("selection"):
        for load in loads[:4]:
            load.wait()
        blocks[me, :, samples:] = selection(
            aperture_ref[...], bucket_ref[...], node_ref[...], gain_ref[...], nodes, half
        ).astype(jnp.bfloat16)
        loads[4].wait()

    with jax.named_scope("entry_barrier"):
        pl.semaphore_wait(barrier, len(partners))

    started = []

    def block_copy(slot, lane, to):
        return pltpu.make_async_remote_copy(
            src_ref=blocks.at[slot],
            dst_ref=blocks.at[slot],
            send_sem=send_sem.at[lane, slot],
            recv_sem=recv_sem.at[slot],
            device_id=(group, to),
            device_id_type=MESH,
        )

    def send(slot, lane, to):
        copy = block_copy(slot, lane, to)
        copy.start()
        started.append(copy)

    def receive(slot, source):
        block_copy(slot, 0, source).wait_recv()

    first_y, first_c = size_z - 1, size_z + size_y - 2

    def send_y(slot):
        for k, to in enumerate(line_y):
            send(slot, first_y + k, index(z, to, core))

    def send_c(slot):
        for k, to in enumerate(line_c):
            send(slot, first_c + k, index(z, y, to))

    for k, to in enumerate(line_z):
        send(me, k, index(to, y, core))
    send_y(me)
    send_c(me)
    table_copies = []
    for load in loads[5:]:
        load.wait()
    for r, other in enumerate(others):
        for which, (source, landing) in enumerate(((travel_ref, travels), (spread_ref, spreads))):
            copy = pltpu.make_async_remote_copy(
                src_ref=source,
                dst_ref=landing.at[group],
                send_sem=table_send.at[which, r],
                recv_sem=table_recv.at[which, group],
                device_id=(other, me),
                device_id_type=MESH,
            )
            copy.start()
            table_copies.append(copy)

    plane = size_y * size_c
    total = plane * count

    def add_plane(at_z, first):
        mine = pl.ds(at_z * plane, plane)
        chosen = blocks[mine, :, samples:].reshape(total, 2 * half).astype(jnp.float32)
        lane = lax.broadcasted_iota(jnp.int32, (1, 2 * half), 1)
        weight = jnp.sum(jnp.where(lane == me, chosen, 0.0), axis=1, keepdims=True)
        row = jnp.sum(jnp.where(lane == me + half, chosen, 0.0), axis=1, keepdims=True)
        rows = lax.broadcasted_iota(jnp.int32, (1, FILTERS * nodes), 1).astype(jnp.float32)
        member = jnp.where(row == rows, weight, 0.0).astype(jnp.bfloat16)
        added = lax.dot_general(
            member,
            blocks[mine, :, :samples].reshape(total, samples),
            (((0,), (0,)), ((), ())),
            preferred_element_type=jnp.float32,
        )
        if first:
            total_ref[...] = added
        else:
            total_ref[...] += added

    def from_z(at_z):
        slot = index(at_z, y, core)
        receive(slot, slot)
        send_y(slot)
        send_c(slot)

    def from_y(at_z):
        for at_y in line_y:
            slot = index(at_z, at_y, core)
            receive(slot, slot)
            send_c(slot)

    def from_c(at_z, first):
        for at_c in line_c:
            for at_y in [y, *line_y]:
                slot = index(at_z, at_y, at_c)
                receive(slot, index(z, y, at_c))
        add_plane(at_z, first)

    planes = [z, *line_z]
    for k in range(size_z + 2):
        if 1 <= k < size_z:
            from_z(planes[k])
        if 1 <= k <= size_z:
            from_y(planes[k - 1])
        if k >= 2:
            from_c(planes[k - 2], k == 2)
    stacked = total_ref[...]
    with jax.named_scope("triangle_filter"):
        width = samples + LANES
        stacked = jnp.concatenate([stacked, jnp.zeros((FILTERS * nodes, LANES), jnp.float32)], axis=1)
        by_bucket = [stacked[b * nodes : (b + 1) * nodes] for b in range(FILTERS)]
        stack = None
        for lag in range(MAX_LAG + 1):
            mixed = None
            for b in range(FILTERS):
                if (level := triangle(b, lag)) > 0:
                    term = by_bucket[b] * level
                    mixed = term if mixed is None else mixed + term
            if lag == 0:
                stack = mixed
            else:
                stack = stack + (pltpu.roll(mixed, lag, 1) + pltpu.roll(mixed, width - lag, 1))
        upper = pltpu.roll(stack, width - 1, 1)[:, :samples]
        stack = stack[:, :samples]

    with jax.named_scope("other_image"):
        part_copies = []
        for r, other in enumerate(others):
            for which, landing in enumerate((travels, spreads)):
                pltpu.make_async_remote_copy(
                    src_ref=landing.at[other],
                    dst_ref=landing.at[other],
                    send_sem=table_send.at[which, r],
                    recv_sem=table_recv.at[which, other],
                    device_id=(other, me),
                    device_id_type=MESH,
                ).wait_recv()
            outgoing[r] = partial_image(stack, upper, travels[other], spreads[other])
            copy = pltpu.make_async_remote_copy(
                src_ref=outgoing.at[r],
                dst_ref=parts.at[group],
                send_sem=part_send.at[r],
                recv_sem=part_recv.at[group],
                device_id=(other, me),
                device_id_type=MESH,
            )
            copy.start()
            part_copies.append(copy)
    with jax.named_scope("own_image"):
        image = partial_image(stack, upper, travels[group], spreads[group])
    with jax.named_scope("last_waits"):
        for copy in started:
            copy.wait_send()
        for copy in table_copies:
            copy.wait_send()
        for r, other in enumerate(others):
            pltpu.make_async_remote_copy(
                src_ref=outgoing.at[r],
                dst_ref=parts.at[other],
                send_sem=part_send.at[r],
                recv_sem=part_recv.at[other],
                device_id=(other, me),
                device_id_type=MESH,
            ).wait_recv()
            image = image + parts[other]
        for copy in part_copies:
            copy.wait_send()
    out_ref[...] = image * scale


def per_device(traces, aperture, bucket, table_node, entry_gain, travel, spread):
    tiles = lax.axis_size("image")
    groups = lax.axis_size("table")
    count, samples = traces.shape
    nodes, cells = travel.shape[1], travel.shape[2]
    half = -(-tiles // (LANES // 2)) * (LANES // 2)
    sizes = split_axis(tiles)
    scale = 1.0 / math.sqrt(count * groups * aperture.shape[1])
    vmem = pl.BlockSpec(memory_space=pltpu.VMEM)
    whole = pl.BlockSpec(memory_space=pl.ANY)
    return pl.pallas_call(
        functools.partial(kernel, sizes, groups, half, scale),
        out_shape=jax.ShapeDtypeStruct((1, cells), jnp.float32),
        in_specs=[whole] * 7,
        out_specs=vmem,
        scratch_shapes=[
            pltpu.VMEM(aperture.shape[::-1], jnp.int32),
            pltpu.VMEM((1, count), jnp.int32),
            pltpu.VMEM(table_node.shape[::-1], jnp.int32),
            pltpu.VMEM(entry_gain.shape[::-1], jnp.bfloat16),
            pltpu.VMEM((tiles, count, samples + 2 * half), jnp.bfloat16),
            pltpu.VMEM((groups, nodes, cells), jnp.float32),
            pltpu.VMEM((groups, nodes, cells), jnp.float32),
            pltpu.VMEM((groups, 1, cells), jnp.float32),
            pltpu.VMEM((max(groups - 1, 1), 1, cells), jnp.float32),
            pltpu.VMEM((FILTERS * nodes, samples), jnp.float32),
            pltpu.SemaphoreType.DMA((7,)),
            pltpu.SemaphoreType.DMA((max(sum(sizes) - 3, 1), tiles)),
            pltpu.SemaphoreType.DMA((tiles,)),
            pltpu.SemaphoreType.DMA((2, max(groups - 1, 1))),
            pltpu.SemaphoreType.DMA((2, groups)),
            pltpu.SemaphoreType.DMA((max(groups - 1, 1),)),
            pltpu.SemaphoreType.DMA((groups,)),
        ],
        compiler_params=pltpu.CompilerParams(
            collective_id=0, has_side_effects=True, vmem_limit_bytes=56 * 1024 * 1024
        ),
        cost_estimate=pl.CostEstimate(flops=10**8, bytes_accessed=10**6, transcendentals=0),
    )(aperture.T, bucket.reshape(1, count), table_node.T, entry_gain.T, traces, travel[0], spread[0])


def solution(mesh):
    in_specs = (
        P(("table", "image"), None),
        P(("table", "image"), None),
        P(("table", "image")),
        P(("table", "image"), None),
        P(("table", "image"), None),
        P("image", None, "table"),
        P("image", None, "table"),
    )
    out_specs = P("image", "table")
    return jax.shard_map(
        per_device, mesh=mesh, in_specs=in_specs, out_specs=out_specs, check_vma=False
    )
```

```python
import functools
import math

import jax
import jax.numpy as jnp
from jax import lax
from jax.experimental import pallas as pl
from jax.experimental.pallas import tpu as pltpu
from jax.sharding import PartitionSpec as P

LANES = 128
FILTERS = 4
MAX_LAG = 7
MESH = pl.DeviceIdType.MESH


def split_axis(count):
    if count == 16:
        return (4, 2, 2)
    root = math.isqrt(count)
    if root * root == count:
        return (root, root, 1)
    return (count, 1, 1)


def peers(size, at):
    found = []
    for step in range(1, size):
        if size & (size - 1):
            found.append(lax.rem(at + step, size))
            continue
        to, bit = at, 1
        while bit <= step:
            if step & bit:
                to = to + bit * (1 - 2 * lax.rem(to // bit, 2))
            bit *= 2
        found.append(to)
    return found


def eye_column(row, count):
    across = lax.broadcasted_iota(jnp.int32, (count, count), 1)
    down = lax.broadcasted_iota(jnp.int32, (count, count), 0)
    return jnp.sum(jnp.where(across == down, row, 0.0), axis=1, keepdims=True)


def selection(aperture, bucket, node, gain, nodes, half):
    count = aperture.shape[1]
    lane = lax.broadcasted_iota(jnp.int32, (count, 2 * half), 1)
    low = lane < half
    tile = jnp.where(low, lane, lane - half).astype(jnp.float32)
    offset = eye_column(bucket.astype(jnp.float32) * nodes, count)
    total = jnp.zeros((count, 2 * half), jnp.float32)
    for a in range(aperture.shape[0]):
        named = eye_column(aperture[a : a + 1].astype(jnp.float32), count)
        row = eye_column(node[a : a + 1].astype(jnp.float32), count) + offset
        weight = eye_column(gain[a : a + 1].astype(jnp.float32), count)
        total = total + jnp.where(named == tile, jnp.where(low, weight, row), 0.0)
    return total


def triangle(bucket, lag):
    half = 2 + 2 * bucket
    return max(half - lag, 0) / (half * half)


def partial_image(stack, upper, travel, spread):
    floor_value = jnp.floor(travel)
    fraction = travel - floor_value
    lower = floor_value.astype(jnp.int32)
    chunk = lax.shift_right_logical(lower, 7)
    inner = jnp.bitwise_and(lower, LANES - 1)
    pieces = []
    for c in range(travel.shape[1] // LANES):
        cells = slice(c * LANES, (c + 1) * LANES)
        here, within = chunk[:, cells], inner[:, cells]
        low = jnp.zeros(here.shape, jnp.float32)
        high = jnp.zeros(here.shape, jnp.float32)
        for k in range(stack.shape[1] // LANES):
            samples = slice(k * LANES, (k + 1) * LANES)
            mine = here == k
            picked = jnp.take_along_axis(stack[:, samples], within, axis=1, mode="promise_in_bounds")
            above = jnp.take_along_axis(upper[:, samples], within, axis=1, mode="promise_in_bounds")
            low = jnp.where(mine, picked, low)
            high = jnp.where(mine, above, high)
        part = fraction[:, cells]
        value = spread[:, cells] * ((1.0 - part) * low + part * high)
        pieces.append(jnp.sum(value, axis=0, keepdims=True))
    return jnp.concatenate(pieces, axis=1)


def kernel(
    sizes, groups, half, scale,
    aperture_hbm, bucket_hbm, node_hbm, gain_hbm, traces_ref, travel_ref, spread_ref,
    out_ref,
    aperture_ref, bucket_ref, node_ref, gain_ref,
    blocks, travels, spreads, parts, outgoing, total_ref,
    load_sem, send_sem, recv_sem, table_send, table_recv, part_send, part_recv,
):
    size_z, size_y, size_c = sizes
    me = lax.axis_index("image")
    group = lax.axis_index("table")
    z = me // (size_y * size_c)
    y = lax.rem(me // size_c, size_y)
    core = lax.rem(me, size_c)
    count, samples = traces_ref.shape
    nodes = travel_ref.shape[0]
    cells = travel_ref.shape[1]

    def index(at_z, at_y, at_c):
        return (at_z * size_y + at_y) * size_c + at_c

    home = (z * size_c + core) * size_y + y
    loads = [
        pltpu.make_async_copy(source, landing, load_sem.at[k])
        for k, (source, landing) in enumerate((
            (aperture_hbm, aperture_ref), (bucket_hbm, bucket_ref), (node_hbm, node_ref), (gain_hbm, gain_ref),
            (traces_ref, blocks.at[home, :, pl.ds(0, samples)]),
            (travel_ref, travels.at[group]), (spread_ref, spreads.at[group]),
        ))
    ]
    for load in loads:
        load.start()

    def place(at_z, at_y, at_c):
        return (at_z * size_c + at_c) * size_y + at_y

    line_z, line_y, line_c = peers(size_z, z), peers(size_y, y), peers(size_c, core)
    others = [lax.rem(group + r, groups) for r in range(1, groups)]

    barrier = pltpu.get_barrier_semaphore()
    if size_z == 4:
        line_z = [line_z[0], line_z[2], line_z[1]]
    partners = [(group, index(to, y, core)) for to in line_z]
    partners += [(group, index(z, to, core)) for to in line_y]
    partners += [(group, index(z, y, to)) for to in line_c]
    partners += [(other, me) for other in others]
    for partner in partners:
        pl.semaphore_signal(barrier, inc=1, device_id=partner, device_id_type=MESH)

    with jax.named_scope("selection"):
        for load in loads[:4]:
            load.wait()
        blocks[home, :, samples:] = selection(
            aperture_ref[...], bucket_ref[...], node_ref[...], gain_ref[...], nodes, half
        ).astype(jnp.bfloat16)
        loads[4].wait()

    with jax.named_scope("entry_barrier"):
        pl.semaphore_wait(barrier, len(partners))

    started = []

    def block_copy(slot, lane, to):
        return pltpu.make_async_remote_copy(
            src_ref=blocks.at[slot],
            dst_ref=blocks.at[slot],
            send_sem=send_sem.at[lane, slot],
            recv_sem=recv_sem.at[slot],
            device_id=(group, to),
            device_id_type=MESH,
        )

    def send(slot, lane, to):
        copy = block_copy(slot, lane, to)
        copy.start()
        started.append(copy)

    def receive(slot, source):
        block_copy(slot, 0, source).wait_recv()

    def line_copy(at_z, at_c, lane, to):
        first = place(at_z, 0, at_c)
        return pltpu.make_async_remote_copy(
            src_ref=blocks.at[pl.ds(first, size_y)],
            dst_ref=blocks.at[pl.ds(first, size_y)],
            send_sem=send_sem.at[lane, first],
            recv_sem=recv_sem.at[first],
            device_id=(group, to),
            device_id_type=MESH,
        )

    first_y, first_c = size_z - 1, size_z + size_y - 2

    def send_y(slot):
        for k, to in enumerate(line_y):
            send(slot, first_y + k, index(z, to, core))

    send_y(home)
    for k, to in enumerate(line_z):
        send(home, k, index(to, y, core))
    table_copies = []
    for r, other in enumerate(others):
        for which, (source, landing) in enumerate(((travel_ref, travels), (spread_ref, spreads))):
            copy = pltpu.make_async_remote_copy(
                src_ref=source,
                dst_ref=landing.at[group],
                send_sem=table_send.at[which, r],
                recv_sem=table_recv.at[which, group],
                device_id=(other, me),
                device_id_type=MESH,
            )
            copy.start()
            table_copies.append(copy)

    plane = size_y * size_c
    total = plane * count

    def add_plane(at_z, first):
        mine = pl.ds(at_z * plane, plane)
        chosen = blocks[mine, :, samples:].reshape(total, 2 * half).astype(jnp.float32)
        lane = lax.broadcasted_iota(jnp.int32, (1, 2 * half), 1)
        weight = jnp.sum(jnp.where(lane == me, chosen, 0.0), axis=1, keepdims=True)
        row = jnp.sum(jnp.where(lane == me + half, chosen, 0.0), axis=1, keepdims=True)
        rows = lax.broadcasted_iota(jnp.int32, (1, FILTERS * nodes), 1).astype(jnp.float32)
        member = jnp.where(row == rows, weight, 0.0).astype(jnp.bfloat16)
        added = lax.dot_general(
            member,
            blocks[mine, :, :samples].reshape(total, samples),
            (((0,), (0,)), ((), ())),
            preferred_element_type=jnp.float32,
        )
        if first:
            total_ref[...] = added
        else:
            total_ref[...] += added

    def from_z(at_z):
        slot = place(at_z, y, core)
        receive(slot, index(at_z, y, core))
        send_y(slot)

    def from_y(at_z):
        for at_y in line_y:
            receive(place(at_z, at_y, core), index(z, at_y, core))
        for k, to in enumerate(line_c):
            copy = line_copy(at_z, core, first_c + k, index(z, y, to))
            copy.start()
            started.append(copy)

    def from_c(at_z, first):
        for at_c in line_c:
            line_copy(at_z, at_c, 0, index(z, y, at_c)).wait_recv()
        add_plane(at_z, first)

    planes = [z, *line_z]
    for k in range(size_z + 2):
        if 1 <= k < size_z:
            from_z(planes[k])
        if 1 <= k <= size_z:
            from_y(planes[k - 1])
        if k >= 2:
            from_c(planes[k - 2], k == 2)
    stacked = total_ref[...]
    with jax.named_scope("triangle_filter"):
        width = samples + LANES
        stacked = jnp.concatenate([stacked, jnp.zeros((FILTERS * nodes, LANES), jnp.float32)], axis=1)
        by_bucket = [stacked[b * nodes : (b + 1) * nodes] for b in range(FILTERS)]
        stack = None
        for lag in range(MAX_LAG + 1):
            mixed = None
            for b in range(FILTERS):
                if (level := triangle(b, lag)) > 0:
                    term = by_bucket[b] * level
                    mixed = term if mixed is None else mixed + term
            if lag == 0:
                stack = mixed
            else:
                stack = stack + (pltpu.roll(mixed, lag, 1) + pltpu.roll(mixed, width - lag, 1))
        upper = pltpu.roll(stack, width - 1, 1)[:, :samples]
        stack = stack[:, :samples]

    with jax.named_scope("other_image"):
        part_copies = []
        for r, other in enumerate(others):
            for which, landing in enumerate((travels, spreads)):
                pltpu.make_async_remote_copy(
                    src_ref=landing.at[other],
                    dst_ref=landing.at[other],
                    send_sem=table_send.at[which, r],
                    recv_sem=table_recv.at[which, other],
                    device_id=(other, me),
                    device_id_type=MESH,
                ).wait_recv()
            outgoing[r] = partial_image(stack, upper, travels[other], spreads[other])
            copy = pltpu.make_async_remote_copy(
                src_ref=outgoing.at[r],
                dst_ref=parts.at[group],
                send_sem=part_send.at[r],
                recv_sem=part_recv.at[group],
                device_id=(other, me),
                device_id_type=MESH,
            )
            copy.start()
            part_copies.append(copy)
    with jax.named_scope("own_image"):
        for load in loads[5:]:
            load.wait()
        image = partial_image(stack, upper, travels[group], spreads[group])
    with jax.named_scope("last_waits"):
        for copy in started:
            copy.wait_send()
        for copy in table_copies:
            copy.wait_send()
        for r, other in enumerate(others):
            pltpu.make_async_remote_copy(
                src_ref=outgoing.at[r],
                dst_ref=parts.at[other],
                send_sem=part_send.at[r],
                recv_sem=part_recv.at[other],
                device_id=(other, me),
                device_id_type=MESH,
            ).wait_recv()
            image = image + parts[other]
        for copy in part_copies:
            copy.wait_send()
    out_ref[...] = image * scale


def per_device(traces, aperture, bucket, table_node, entry_gain, travel, spread):
    tiles = lax.axis_size("image")
    groups = lax.axis_size("table")
    count, samples = traces.shape
    nodes, cells = travel.shape[1], travel.shape[2]
    half = -(-tiles // (LANES // 2)) * (LANES // 2)
    sizes = split_axis(tiles)
    scale = 1.0 / math.sqrt(count * groups * aperture.shape[1])
    vmem = pl.BlockSpec(memory_space=pltpu.VMEM)
    whole = pl.BlockSpec(memory_space=pl.ANY)
    return pl.pallas_call(
        functools.partial(kernel, sizes, groups, half, scale),
        out_shape=jax.ShapeDtypeStruct((1, cells), jnp.float32),
        in_specs=[whole] * 7,
        out_specs=vmem,
        scratch_shapes=[
            pltpu.VMEM(aperture.shape[::-1], jnp.int32),
            pltpu.VMEM((1, count), jnp.int32),
            pltpu.VMEM(table_node.shape[::-1], jnp.int32),
            pltpu.VMEM(entry_gain.shape[::-1], jnp.bfloat16),
            pltpu.VMEM((tiles, count, samples + 2 * half), jnp.bfloat16),
            pltpu.VMEM((groups, nodes, cells), jnp.float32),
            pltpu.VMEM((groups, nodes, cells), jnp.float32),
            pltpu.VMEM((groups, 1, cells), jnp.float32),
            pltpu.VMEM((max(groups - 1, 1), 1, cells), jnp.float32),
            pltpu.VMEM((FILTERS * nodes, samples), jnp.float32),
            pltpu.SemaphoreType.DMA((7,)),
            pltpu.SemaphoreType.DMA((max(sum(sizes) - 3, 1), tiles)),
            pltpu.SemaphoreType.DMA((tiles,)),
            pltpu.SemaphoreType.DMA((2, max(groups - 1, 1))),
            pltpu.SemaphoreType.DMA((2, groups)),
            pltpu.SemaphoreType.DMA((max(groups - 1, 1),)),
            pltpu.SemaphoreType.DMA((groups,)),
        ],
        compiler_params=pltpu.CompilerParams(
            collective_id=0, has_side_effects=True, vmem_limit_bytes=56 * 1024 * 1024
        ),
        cost_estimate=pl.CostEstimate(flops=10**8, bytes_accessed=10**6, transcendentals=0),
    )(aperture.T, bucket.reshape(1, count), table_node.T, entry_gain.T, traces, travel[0], spread[0])


def solution(mesh):
    in_specs = (
        P(("table", "image"), None),
        P(("table", "image"), None),
        P(("table", "image")),
        P(("table", "image"), None),
        P(("table", "image"), None),
        P("image", None, "table"),
        P("image", None, "table"),
    )
    out_specs = P("image", "table")
    return jax.shard_map(
        per_device, mesh=mesh, in_specs=in_specs, out_specs=out_specs, check_vma=False
    )
```
